32 devices in a mesh: section: 2 (over x), batch: 4 (over z), tensor: 4 (over y, core).
Axes of the slice: x: 2, y: 2, z: 4, core: 2. Of those that a mesh axis runs over, the one named last changes fastest.
Arguments:
- clips: bfloat16 [8, 1024, 768], P('batch', 'tensor'), may hold values from -32 to 32
- group_clips: int32 [4], P('batch'), may hold values from 1 to 2, as said below
- ln1_gain: float32 [2, 768], P('section'), may hold values from 0.5 to 1.5
- ln1_bias: float32 [2, 768], P('section'), may hold values from -4 to 4
- qkv_weight: bfloat16 [2, 768, 3, 768], P('section', None, None, 'tensor'), may hold values from -0.21875 to 0.21875
- q_bias: float32 [2, 768], P('section', 'tensor'), may hold values from -6 to 6
- v_bias: float32 [2, 768], P('section', 'tensor'), may hold values from -6 to 6
- out_weight: bfloat16 [2, 768, 768], P('section', 'tensor'), may hold values from -0.875 to 0.875
- out_bias: float32 [2, 768], P('section'), may hold values from -4 to 4
- ln2_gain: float32 [2, 768], P('section'), may hold values from 0.5 to 1.5
- ln2_bias: float32 [2, 768], P('section'), may hold values from -4 to 4
- up_weight: bfloat16 [2, 768, 3072], P('section', None, 'tensor'), may hold values from -0.21875 to 0.21875
- up_bias: float32 [2, 3072], P('section', 'tensor'), may hold values from -6 to 6
- down_weight: bfloat16 [2, 3072, 768], P('section', 'tensor'), may hold values from -0.109375 to 0.109375
- down_bias: float32 [2, 768], P('section'), may hold values from -4 to 4
- cotangent: bfloat16 [8, 1024, 768], P('batch', 'tensor'), may hold values from -6 to 6
Outputs:
- states: bfloat16 [2, 8, 1024, 768], P('section', 'batch', 'tensor')
- state_grads: float32 [2, 8, 1024, 768], P('section', 'batch', 'tensor')
- ln1_gain_grad: float32 [2, 768], P('section')
- ln1_bias_grad: float32 [2, 768], P('section')
- qkv_weight_grad: float32 [2, 768, 3, 768], P('section', None, None, 'tensor')
- q_bias_grad: float32 [2, 768], P('section', 'tensor')
- v_bias_grad: float32 [2, 768], P('section', 'tensor')
- out_weight_grad: float32 [2, 768, 768], P('section', 'tensor')
- out_bias_grad: float32 [2, 768], P('section')
- ln2_gain_grad: float32 [2, 768], P('section')
- ln2_bias_grad: float32 [2, 768], P('section')
- up_weight_grad: float32 [2, 768, 3072], P('section', None, 'tensor')
- up_bias_grad: float32 [2, 3072], P('section', 'tensor')
- down_weight_grad: float32 [2, 3072, 768], P('section', 'tensor')
- down_bias_grad: float32 [2, 768], P('section')
The draws below stay inside these ranges and needn't reach their ends.
Inputs may be any that keep to these rules, and one draw needn't show every extreme that they name: group_clips[g] of the group's 2 slots hold clips, the first ones; some group holds 2.
All inputs are finite; a program needn't handle non-finite values.
Results may differ from the reference program's by a relative error of at most 0.018.
Values may be sent and summed in bfloat16 or wider, within the bound.
A program may use at most 192 MiB of HBM per device.

```python
import jax
import jax.numpy as jnp
from jax import lax

D = 768
HEADS = 12
HD = 64
FF = 3072
LEN = 1024
QBLOCK = 512
MICRO = 2
LAYERS = 2
SLOTS = 8


def draw_clips(key, part):
    key = jax.random.fold_in(key, 11)
    noise_key, bias_key, scale_key = jax.random.split(key, 3)
    shape = (SLOTS, LEN, D)
    order = jnp.arange(SLOTS)[:, None] * LEN + jnp.arange(LEN)[None, :]
    position = (order.astype(jnp.float32) / (SLOTS * LEN))[:, :, None]
    feature_bias = 0.5 * jnp.clip(jax.random.normal(bias_key, (D,), jnp.float32), -3.0, 3.0)
    feature_scale = jnp.exp(jax.random.uniform(scale_key, (D,), jnp.float32, -0.5, 0.5))
    noise = jnp.clip(jax.random.normal(noise_key, shape, jnp.float32), -4.0, 4.0)
    rising = 1.0 + 2.0 * position
    offset = 3.0 * position - 1.5
    return (offset + rising * feature_scale * (feature_bias + noise)).astype(jnp.bfloat16)


def draw_group_clips(key, part):
    key = jax.random.fold_in(key, 23)
    count_key, pick_key = jax.random.split(key)
    groups = SLOTS // MICRO
    counts = jax.random.randint(count_key, (groups,), 1, MICRO + 1)
    chosen = jax.random.randint(pick_key, (), 0, groups)
    return jnp.where(jnp.arange(groups) == chosen, MICRO, counts).astype(jnp.int32)


def shard_levels(own_key, shape, shards, smallest, high):
    factor_of = 1.0
    for axis_at, blocks in shards:
        draws = jax.random.uniform(jax.random.fold_in(jax.random.fold_in(own_key, 6), axis_at), (blocks,), jnp.float32, smallest / len(shards), high / len(shards))
        factor_of = factor_of * jnp.repeat(jnp.exp(draws), shape[axis_at] // blocks).reshape((-1,) + (1,) * (len(shape) - 1 - axis_at))
    return factor_of


def scatter_about(stream_key, dims, scale, limit, pieces=(), kind=jnp.bfloat16):
    drawn = scale * jax.random.normal(stream_key, dims, jnp.float32)
    if pieces:
        drawn = drawn * shard_levels(stream_key, dims, pieces, -0.22, 0.18)
    return jnp.clip(drawn, -limit, limit).astype(kind)


def setup_inputs(seed: int = 0) -> dict:
    splits = jax.random.split(jax.random.key(seed), 17)
    clips = draw_clips(jax.random.fold_in(splits[16], 71), 0)
    group_clips = draw_group_clips(jax.random.fold_in(splits[16], 71), 0)
    ln1_gain = jnp.clip(1.0 + 0.1 * jax.random.normal(splits[2], (LAYERS, D), jnp.float32), 0.5, 1.5)
    ln1_bias = scatter_about(splits[3], (LAYERS, D), 0.3, 4.0, ((0, 2),), jnp.float32)
    qkv_weight = scatter_about(splits[4], (LAYERS, D, 3, D), D ** -0.5, 0.21875, ((0, 2), (3, 4)))
    q_bias = scatter_about(splits[5], (LAYERS, D), 0.5, 6.0, ((0, 2), (1, 4)), jnp.float32)
    v_bias = scatter_about(splits[6], (LAYERS, D), 0.5, 6.0, ((0, 2), (1, 4)), jnp.float32)
    out_weight = scatter_about(splits[7], (LAYERS, D, D), (D // 16) ** -0.5, 0.875, ((0, 2), (1, 4)))
    out_bias = scatter_about(splits[8], (LAYERS, D), 0.3, 4.0, ((0, 2),), jnp.float32)
    ln2_gain = jnp.clip(1.0 + 0.1 * jax.random.normal(splits[9], (LAYERS, D), jnp.float32), 0.5, 1.5)
    ln2_bias = scatter_about(splits[10], (LAYERS, D), 0.3, 4.0, ((0, 2),), jnp.float32)
    up_weight = scatter_about(splits[11], (LAYERS, D, FF), D ** -0.5, 0.21875, ((0, 2), (2, 4)))
    up_bias = scatter_about(splits[12], (LAYERS, FF), 0.5, 6.0, ((0, 2), (1, 4)), jnp.float32)
    down_weight = scatter_about(splits[13], (LAYERS, FF, D), FF ** -0.5, 0.109375, ((0, 2), (1, 4)))
    down_bias = scatter_about(splits[14], (LAYERS, D), 0.3, 4.0, ((0, 2),), jnp.float32)
    cotangent = scatter_about(splits[15], (SLOTS, LEN, D), 1.0, 6.0, ((0, 4), (1, 4)))
    return dict(clips=clips, group_clips=group_clips, ln1_gain=ln1_gain, ln1_bias=ln1_bias, qkv_weight=qkv_weight, q_bias=q_bias, v_bias=v_bias, out_weight=out_weight, out_bias=out_bias, ln2_gain=ln2_gain, ln2_bias=ln2_bias, up_weight=up_weight, up_bias=up_bias, down_weight=down_weight, down_bias=down_bias, cotangent=cotangent)


@jax.custom_vjp
def low(v):
    return lax.optimization_barrier(v.astype(jnp.bfloat16)).astype(jnp.float32)

@jax.custom_vjp
def low_back(v):
    return v

def low_keep(v):
    return (low(v), None)

def low_pass(kept, grad):
    return (grad,)

def back_keep(v):
    return (v, None)

def back_low(kept, grad):
    return (low(grad),)
low.defvjp(low_keep, low_pass)
low_back.defvjp(back_keep, back_low)
highest = lax.Precision.HIGHEST

def norm_apply(inputs, gain, offset):
    center = lax.optimization_barrier(jnp.mean(inputs, axis=-1, keepdims=True))
    shifted = inputs - center
    spread = lax.optimization_barrier(jnp.mean(shifted * shifted, axis=-1, keepdims=True))
    return shifted * lax.rsqrt(spread + 1e-06) * gain + offset

def block(inputs, weight_set, layer_index):
    gain_one, offset_one, qkv_matrix, bias_query, bias_value, out_matrix, out_shift, gain_two, offset_two, up_matrix, up_shift, down_matrix, down_shift = [item[layer_index] for item in weight_set]
    normed = low(norm_apply(inputs, gain_one, offset_one))
    bias_all = jnp.stack([bias_query, jnp.zeros_like(bias_query), bias_value])
    projected = jnp.einsum('td,dcf->tcf', normed, qkv_matrix, precision=highest) + bias_all
    projected = low_back(low(projected))
    queries = projected[:, 0].reshape(LEN // QBLOCK, QBLOCK, HEADS, HD)
    keys_all = projected[:, 1].reshape(LEN, HEADS, HD)
    values_all = projected[:, 2].reshape(LEN, HEADS, HD)
    score_scale = HD ** (-0.5)

    def attend(query_block):
        scores = low_back(jnp.einsum('qhd,khd->hqk', query_block, keys_all, precision=highest) * score_scale)
        largest = lax.optimization_barrier(jnp.max(scores, axis=-1, keepdims=True))
        exponent = jnp.exp(scores - largest)
        soft_weights = low(exponent / lax.optimization_barrier(jnp.sum(exponent, axis=-1, keepdims=True)))
        return jnp.einsum('hqk,khd->qhd', soft_weights, values_all, precision=highest)
    attended = lax.map(jax.checkpoint(attend), queries).reshape(LEN, D)
    attended = low_back(low(attended))
    attn_branch = low_back(jnp.dot(attended, out_matrix, precision=highest) + out_shift)
    hidden = inputs + attn_branch
    normed_two = low(norm_apply(hidden, gain_two, offset_two))
    before = low_back(jnp.dot(normed_two, up_matrix, precision=highest) + up_shift)
    active = low(jax.nn.gelu(before, approximate=False))
    branch = low_back(jnp.dot(active, down_matrix, precision=highest) + down_shift)
    return hidden + branch

def reference(clips, group_clips, ln1_gain, ln1_bias, qkv_weight, q_bias, v_bias, out_weight, out_bias, ln2_gain, ln2_bias, up_weight, up_bias, down_weight, down_bias, cotangent):
    valid_slots = (jnp.arange(MICRO)[None, :] < group_clips[:, None]).reshape(SLOTS).astype(jnp.float32)
    valid_rows = valid_slots[:, None, None]
    token_total = jnp.sum(valid_slots) * LEN
    weights = tuple((item.astype(jnp.float32) for item in (ln1_gain, ln1_bias, qkv_weight, q_bias, v_bias, out_weight, out_bias, ln2_gain, ln2_bias, up_weight, up_bias, down_weight, down_bias)))
    raw_clips = clips.astype(jnp.float32)
    probe_input = jnp.zeros((SLOTS, LEN, D), jnp.float32)

    def forward(raw_input, probe_part, weight_set):
        center = lax.optimization_barrier(jnp.sum(raw_input * valid_rows, axis=(0, 1))) / token_total
        shifted = raw_input - center
        spread = lax.optimization_barrier(jnp.sum(shifted * shifted * valid_rows, axis=(0, 1))) / token_total
        standard = shifted * lax.rsqrt(spread + 1e-05)

        def one_clip(clip_parts):
            clip_input, clip_probe = clip_parts
            first_out = low(block(clip_input, weight_set, 0))
            second_out = block(low_back(first_out) + clip_probe, weight_set, 1)
            return (first_out, second_out)
        first_all, second_all = lax.map(jax.checkpoint(one_clip), (standard, probe_part))
        return jnp.stack([first_all * valid_rows, second_all * valid_rows])
    states, pull_back = jax.vjp(forward, raw_clips, probe_input, weights)
    cot_pair = jnp.stack([jnp.zeros((SLOTS, LEN, D), jnp.float32), cotangent.astype(jnp.float32)])
    grad_clips, grad_probe, grad_weights = pull_back(cot_pair)
    return (states.astype(jnp.bfloat16), jnp.stack([grad_clips, grad_probe]), grad_weights[0], grad_weights[1], grad_weights[2], grad_weights[3], grad_weights[4], grad_weights[5], grad_weights[6], grad_weights[7], grad_weights[8], grad_weights[9], grad_weights[10], grad_weights[11], grad_weights[12])
```

```python
import functools

import jax
import jax.numpy as jnp
from jax import lax
from jax.experimental import pallas as pl
from jax.experimental.pallas import tpu as pltpu
from jax.sharding import PartitionSpec as P

HD = 64
BF = jnp.bfloat16
F32 = jnp.float32
NN = (((1,), (0,)), ((), ()))
NT = (((1,), (1,)), ((), ()))
TN = (((0,), (0,)), ((), ()))
MESH = pl.DeviceIdType.MESH


def dot(a, b, dims):
    return lax.dot_general(a, b, dims, preferred_element_type=F32)


def cut(start, stop, step):
    return [(at, min(step, stop - at)) for at in range(start, stop, step)]


def lane_mask(head):
    lane = lax.broadcasted_iota(jnp.int32, (1, 2 * HD), 1)
    return lane < HD if head == 0 else lane >= HD


def normalize(v):
    shifted = v - jnp.mean(v, axis=-1, keepdims=True)
    scale = lax.rsqrt(jnp.mean(shifted * shifted, axis=-1, keepdims=True) + 1e-06)
    return shifted * scale, scale


def norm_back(g, gain, unit, scale):
    t = g * gain
    return scale * (
        t - jnp.mean(t, axis=-1, keepdims=True) - unit * jnp.mean(t * unit, axis=-1, keepdims=True)
    )


def column_sum(v):
    return jnp.sum(v, axis=0, keepdims=True)


def plan(rows, width, head_width, hidden, batches):
    planes = hidden + 16, hidden + 16, 4 * head_width + 16
    depth = max(planes[2], hidden)
    pieces = []
    for which in (0, 1):
        pieces += [(which, at, size) for at, size in cut(0, hidden, 256)]
    pieces += [(2, at, size) for at, size in cut(0, 3 * head_width, head_width)]
    pieces.append((2, 3 * head_width, head_width + 16))
    names = ["in", "bias", "states", "sg"]
    names += [f"{way}{k}" for way in ("wy", "wz") for k in range(8)]
    for kind in ("n1", "n2", "gm", "ga", "o1", "o2", "o3", "o4", "x", "g"):
        names += [kind + "0", kind + "1"]
    for k in range(len(pieces)):
        names += [f"y{k}", f"in{k}", f"out{k}", f"final{k}"]
    for stage in ("a", "b"):
        names += [f"{stage}z{j}" for j in range(1, batches)]
        names += [f"{stage}t{j}" for j in range(1, 4)]
    return depth, pieces, {name: i for i, name in enumerate(names)}


def body(
    dims,
    clips, cot, wq, wo, wu, wd, par, bias_own, bias_send, valid,
    g_out, states, sg, small,
    wqb, wob, wub, wdb, bias_in, stat, statz, statt, sums, sumz, sumt,
    xs, hid, gh, n1, qb, kb, vb, prob, linv, att, att_rest, n2, act, gp, gm, ga, gatt,
    send_a, send_b, recv_a, recv_b, obuf, gxb, gown, gsend, grecv,
    ss, rs, ls, ready,
):
    rows, width, head_width, hidden, batches, pieces, index = dims
    half = 2 * rows
    length = 4 * rows
    heads = 2 * head_width // HD
    pairs = heads // 2
    section = lax.axis_index("section")
    b = lax.axis_index("batch")
    t = lax.axis_index("tensor")
    y, core = t // 2, t % 2
    core_peer = (section, b, 2 * y + 1 - core)
    y_peer = (section, b, 2 * (1 - y) + core)
    x_peer = (1 - section, b, t)
    early = section == 0
    late = section == 1

    def remote(src, dst, name, device, sent=None):
        i = index[name]
        return pltpu.make_async_remote_copy(
            src_ref=src, dst_ref=dst, send_sem=ss.at[index[sent or name]], recv_sem=rs.at[i],
            device_id=device, device_id_type=MESH,
        )

    def local(src, dst, i):
        return pltpu.make_async_copy(src, dst, ls.at[i])

    inb = recv_b
    own_loads = [
        local(clips.at[0], send_a.at[pl.ds(0, rows)], 0),
        local(wq, wqb.at[:, pl.ds(0, head_width)], 1),
        local(wo, wob.at[pl.ds(0, head_width)], 2),
        local(wu, wub.at[0], 3),
        local(wd, wdb.at[0], 4),
        local(clips.at[1], send_a.at[pl.ds(rows, rows)], 7),
    ]
    for load in own_loads:
        load.start()

    @pl.when(early)
    def _():
        local(clips.at[y], inb.at[pl.ds(0, rows)], 5).start()

    @pl.when(late)
    def _():
        local(cot.at[y], inb.at[pl.ds(0, rows)], 5).start()

    barrier = pltpu.get_barrier_semaphore()
    peers = [x_peer]
    peers += [(section, lax.rem(b + j, batches), t) for j in range(1, batches)]
    peers += [(section, b, lax.rem(t + j, 4)) for j in range(1, 4)]
    for peer in peers:
        pl.semaphore_signal(barrier, inc=1, device_id=peer, device_id_type=MESH)

    in_dst = inb.at[pl.ds(rows, rows)]

    z_peer = (section, b + 1 - 2 * lax.rem(b, 2), t)
    fresh = lax.rem(b, 2)
    bias_copy = remote(bias_send, bias_in, "bias", y_peer)
    parts = []
    for source, target, at, size in (
        [(wq.at[c], lambda r, c=c: wqb.at[c, pl.ds(head_width + r[0], r[1])], 0, head_width) for c in range(3)]
        + [(wo, lambda r: wob.at[pl.ds(head_width + r[0], r[1])], 0, head_width)]
        + [(wu, lambda r: wub.at[1, pl.ds(*r)], at, width // 2) for at in (0, width // 2)]
        + [(wd, lambda r: wdb.at[1, pl.ds(*r)], at, hidden // 2) for at in (0, hidden // 2)]
    ):
        parts.append((source, target, at, size // 2))

    def weight_rows(k, turn):
        _, _, at, size = parts[k]
        return pl.multiple_of(at + turn * size, 16), size

    def weight_copy(k):
        source, target, _, _ = parts[k]
        where = weight_rows(k, fresh)
        return remote(source.at[pl.ds(*where)], target(where), f"wy{k}", y_peer)

    def weight_relay(k, turn):
        place = parts[k][1](weight_rows(k, turn))
        return remote(place, place, f"wz{k}", z_peer)

    def relay(*which):
        for k in which:
            weight_copy(k).wait_recv()
            weight_relay(k, fresh).start()

    def arrive(*which):
        for k in which:
            weight_relay(k, 1 - fresh).wait_recv()

    def share_out(stage, block, slots, axis):
        size, me = (batches, b) if axis == "z" else (4, t)
        copies = []
        for j in range(1, size):
            to = lax.rem(me + j, size)
            device = (section, to, t) if axis == "z" else (section, b, to)
            copies.append(remote(block, slots.at[me], f"{stage}{axis}{j}", device))
        for copy in copies:
            copy.start()
        slots[pl.ds(me, 1)] = block[...][None]

        def finish():
            for j in range(1, size):
                origin = lax.rem(me + size - j, size)
                remote(block, slots.at[origin], f"{stage}{axis}{j}", core_peer).wait_recv()
            for copy in copies:
                copy.wait_send()

        return finish

    def store_stats(total, centered, count):
        stat[0:1, :] = total
        stat[1:2, :] = centered
        stat[2:3, :] = count
        stat[3:8, :] = jnp.zeros((5, width), F32)

    def merge_stats(slots):
        blocks = slots[...]
        total = jnp.sum(blocks[:, 0:1, :], axis=0)
        count = jnp.sum(blocks[:, 2:3, :], axis=0)
        away = blocks[:, 0, :] / blocks[:, 2, :] - total / count
        centered = jnp.sum(blocks[:, 1, :] + blocks[:, 2, :] * away * away, axis=0, keepdims=True)
        store_stats(total, centered, count)

    own_loads[0].wait()
    own_loads[5].wait()
    slots_of = [slice(m * rows, (m + 1) * rows) for m in range(2)]
    weight = [valid[m : m + 1, 0:1] for m in range(2)]
    count = rows * (weight[0] + weight[1])
    total = jnp.zeros((1, width), F32)
    for m in range(2):
        total = total + weight[m] * column_sum(send_a[slots_of[m], :].astype(F32))
    centered = jnp.zeros((1, width), F32)
    for m in range(2):
        away = send_a[slots_of[m], :].astype(F32) - total / count
        centered = centered + weight[m] * column_sum(away * away)
    store_stats(total, centered, count + jnp.zeros((1, width), F32))
    pl.semaphore_wait(barrier, len(peers))
    finish = share_out("a", stat, statt, "t")
    bias_copy.start()

    @pl.when(early)
    def _():
        remote(clips.at[1 - y], in_dst, "in", y_peer).start()

    @pl.when(late)
    def _():
        remote(cot.at[1 - y], in_dst, "in", y_peer).start()

    for k in range(len(parts)):
        weight_copy(k).start()

    finish()
    merge_stats(statt)
    finish = share_out("a", stat, statz, "z")
    finish()
    merge_stats(statz)

    @pl.when(early)
    def _():
        relay(0, 1)

    center = stat[0:1, :] / stat[2:3, :]
    inv_spread = lax.rsqrt(stat[1:2, :] / stat[2:3, :] + 1e-05)
    small[8:9, :] = center
    small[9:10, :] = inv_spread
    small[10:11, :] = stat[2:3, :]
    small[11:16, :] = jnp.zeros((5, width), F32)

    local(clips.at[y], inb.at[pl.ds(0, rows)], 5).wait()
    remote(clips.at[0], in_dst, "in", y_peer).wait_recv()
    own_rows = cut(0, half, rows)
    both = [(0, half), (half, half)]

    def share(buffer, kind, i):
        at, size = own_rows[i]
        return remote(
            buffer.at[pl.ds(at, size)], buffer.at[pl.ds(half + at, size)], f"{kind}{i}", core_peer
        )

    def grad_active():
        for at, size in both:
            for j in range(2):
                yield at, size, j, dot(gm[at : at + size, :], wdb[j], NT)

    own_loads[4].wait()

    @pl.when(early)
    def _():
        gp[...] = jnp.ones((2, length, hidden), BF)

    @pl.when(late)
    def _():
        mine = valid[pl.ds(y, 1), 0:1]
        for i, (at, size) in enumerate(own_rows):
            gm[at : at + size, :] = (inb[at : at + size, :].astype(F32) * mine).astype(BF)
            share(gm, "gm", i).start()
        relay(6, 7, 0, 1, 2, 3, 4, 5)
        arrive(6, 7)
        for i in range(2):
            share(gm, "gm", i).wait_recv()
        for at, size, j, value in grad_active():
            gp[j, at : at + size, :] = value.astype(BF)

    for i, (at, size) in enumerate(own_rows):
        r = slice(at, at + size)

        @pl.when(early)
        def _():
            xs[r, :] = (inb[r, :].astype(F32) - center) * inv_spread

        @pl.when(late)
        def _():
            remote(obuf.at[r], obuf.at[r], f"x{i}", x_peer).wait_recv()
            xs[r, :] = obuf[r, :].astype(F32)

        unit, _ = normalize(xs[r, :])
        n1[r, :] = (unit * par[0:1, :] + par[1:2, :]).astype(BF)
        share(n1, "n1", i).start()

    @pl.when(early)
    def _():
        relay(2, 3)

    own_loads[1].wait()
    bias_copy.wait_recv()
    arrive(0, 1, 2)
    shift = bias_own[...] + bias_in[...]
    shift_q = shift[1:2, : 2 * head_width]
    shift_v = shift[2:3, : 2 * head_width]

    def project(r):
        normed = n1[r, :]
        qb[r, :] = ((dot(normed, wqb[0], NT) + shift_q).astype(BF) * jnp.array(HD**-0.5, BF)).astype(BF)
        kb[r, :] = dot(normed, wqb[1], NT).astype(BF)
        vb[r, :] = (dot(normed, wqb[2], NT) + shift_v).astype(BF)

    project(slice(0, half))
    for i in range(2):
        share(n1, "n1", i).wait_recv()
    project(slice(half, length))

    zero = jnp.zeros((), BF)
    for pair in range(pairs):
        cs = slice(pair * 2 * HD, (pair + 1) * 2 * HD)
        for at, size in both:
            r = slice(at, at + size)
            outs = []
            for head in range(2):
                mask = lane_mask(head)
                scores = dot(jnp.where(mask, qb[r, cs], zero), kb[:, cs], NT)
                exponent = jnp.exp(scores - jnp.max(scores, axis=1, keepdims=True)).astype(BF)
                prob[2 * pair + head, r, :] = exponent
                lane = lax.broadcasted_iota(jnp.int32, (1, 2 * HD), 1)
                ones = jnp.where(lane == HD * (1 - head), jnp.ones((), BF), zero)
                result = dot(exponent, jnp.where(mask, vb[:, cs], ones), NN)
                first = HD * (1 - head)
                factor = 1.0 / result[:, first : first + 1]
                linv[r, 2 * pair + head : 2 * pair + head + 1] = factor
                outs.append(result * factor)
            exact = jnp.where(lane_mask(0), outs[0], outs[1])
            near = exact.astype(BF)
            att[r, cs] = near
            att_rest[r, cs] = (exact - near.astype(F32)).astype(BF)
        if pair == 1:

            @pl.when(early)
            def _():
                relay(4)


    def reduce_start(value, i, name, send, recv):
        at, size = own_rows[i]
        send[at : at + size, :] = value.astype(BF)
        remote(send.at[pl.ds(at, size)], recv.at[pl.ds(at, size)], f"{name}{i}", core_peer).start()

    def reduce_end(i, name, send, recv):
        at, size = own_rows[i]
        remote(send.at[pl.ds(at, size)], recv.at[pl.ds(at, size)], f"{name}{i}", core_peer).wait()
        return recv[at : at + size, :].astype(F32)

    own_loads[2].wait()
    arrive(3)
    for i, (at, size) in enumerate(own_rows):
        reduce_start(dot(att[half + at : half + at + size, :], wob[...], NN), i, "o1", send_a, recv_a)
    for i, (at, size) in enumerate(own_rows):
        r = slice(at, at + size)
        partial = dot(att[r, :], wob[...], NN)
        hidden_rows = xs[r, :] + (partial + reduce_end(i, "o1", send_a, recv_a) + par[2:3, :])
        hid[r, :] = hidden_rows
        unit, _ = normalize(hidden_rows)
        n2[r, :] = (unit * par[3:4, :] + par[4:5, :]).astype(BF)
        share(n2, "n2", i).start()

    def up(j, r):
        before = dot(n2[r, :], wub[j], NN) + (bias_own if j == 0 else bias_in)[0:1, :]
        share_of = 0.5 + 0.5 * lax.erf(before * (2.0**-0.5))
        act[j, r, :] = (before * share_of).astype(BF)
        slope = share_of + before * jnp.exp(-0.5 * before * before) * 0.3989422804014327
        gp[j, r, :] = (gp[j, r, :].astype(F32) * slope).astype(BF)

    @pl.when(early)
    def _():
        relay(5)

    own_loads[3].wait()
    up(0, slice(0, half))
    for i in range(2):
        share(n2, "n2", i).wait_recv()
    up(0, slice(half, length))

    @pl.when(early)
    def _():
        relay(6, 7)

    arrive(4, 5)
    up(1, slice(0, half))
    up(1, slice(half, length))

    def down(r):
        return dot(act[0, r, :], wdb[0], NN) + dot(act[1, r, :], wdb[1], NN)

    def finish_forward(send_on):
        for i, (at, size) in enumerate(own_rows):
            reduce_start(down(slice(half + at, half + at + size)), i, "o2", send_b, recv_b)
        for i, (at, size) in enumerate(own_rows):
            r = slice(at, at + size)
            value = down(r) + reduce_end(i, "o2", send_b, recv_b) + par[5:6, :]
            obuf[r, :] = (hid[r, :] + value).astype(BF)
            if send_on:
                part = obuf.at[pl.ds(at, size)]
                remote(part, part, f"x{i}", x_peer).start()

        local(obuf.at[pl.ds(0, rows)], states.at[y], 6).start()
        remote(obuf.at[pl.ds(rows, rows)], states.at[y], "states", y_peer).start()

    inner = jnp.where(b < batches // 2, b + 1, b - 1)
    outer = jnp.where(b < batches // 2, b - 1, b + 1)
    inner_peer, outer_peer = (section, inner, t), (section, outer, t)
    is_end = jnp.logical_or(b == 0, b == batches - 1)
    is_middle = jnp.logical_or(b == batches // 2 - 1, b == batches // 2)
    not_end, not_middle = jnp.logical_not(is_end), jnp.logical_not(is_middle)

    def offer(plane):
        @pl.when(is_middle)
        def _():
            pl.semaphore_signal(ready.at[plane, 0], inc=1, device_id=inner_peer, device_id_type=MESH)

        @pl.when(not_middle)
        def _():
            pl.semaphore_signal(ready.at[plane, 1], inc=1, device_id=inner_peer, device_id_type=MESH)

        @pl.when(not_end)
        def _():
            pl.semaphore_signal(ready.at[plane, 0], inc=1, device_id=outer_peer, device_id_type=MESH)

    def slot(k, outside):
        plane, at, size = pieces[k]
        home = (wdb, wub, prob)[plane]
        return home.at[outside, pl.ds(at, size), pl.ds(0, width)]

    def block(ref, k):
        plane, at, size = pieces[k]
        return ref.at[plane, pl.ds(at, size)]

    def crossing(k):
        return remote(block(gown, k), slot(k, 0), f"in{k}", inner_peer)

    def inward(k):
        return remote(block(gown, k), slot(k, 1), f"out{k}", inner_peer)

    def outward(k):
        return remote(slot(k, 0), slot(k, 0), f"in{k}", outer_peer, f"final{k}")

    def leave(k):
        return local(slot(k, 0), block(g_out, k), 8 + k)

    def add_chips(k):
        plane, at, size = pieces[k]
        r = slice(at, at + size)
        remote(block(gsend, k), block(grecv, k), f"y{k}", y_peer).wait()
        chip = gown[plane, r, :].astype(F32) + grecv[plane, r, :].astype(F32)

        @pl.when(is_end)
        def _():
            gown[plane, r, :] = chip.astype(BF)

        @pl.when(not_end)
        def _():
            inward(k).wait_recv()
            gown[plane, r, :] = (chip + slot(k, 1)[...].astype(F32)).astype(BF)

        if at == 0:
            pl.semaphore_wait(ready.at[plane, 0], 1)

            @pl.when(not_end)
            def _():
                pl.semaphore_wait(ready.at[plane, 1], 1)

        @pl.when(is_middle)
        def _():
            crossing(k).start()

        @pl.when(not_middle)
        def _():
            inward(k).start()

    def pass_on(k):
        @pl.when(not_end)
        def _():
            outward(k).start()

        leave(k).start()

    def add_middle(k):
        plane, at, size = pieces[k]
        crossing(k).wait_recv()
        value = gown[plane, at : at + size, :].astype(F32) + slot(k, 0)[...].astype(F32)
        slot(k, 0)[...] = value.astype(BF)
        pass_on(k)

    def receive(k):
        crossing(k).wait_recv()
        pass_on(k)

    def advance(where, at_ends, inside):
        @pl.when(jnp.logical_and(where, is_end))
        def _():
            for k in at_ends:
                add_chips(k)

        @pl.when(jnp.logical_and(where, not_end))
        def _():
            for kind, k in inside:
                if kind == "A":
                    add_chips(k)
                else:

                    @pl.when(is_middle)
                    def _():
                        add_middle(k)

    def steps(start, stop, lag=1):
        found = []
        for k in range(start, stop):
            found.append(("A", k))
            if k >= lag:
                found.append(("M", k - lag))
        return found

    def send_pieces(which, start, stop):
        for k, (plane, at, size) in enumerate(pieces):
            if plane == which and start <= at < stop:
                part = pl.ds(at, size)
                remote(gsend.at[plane, part], grecv.at[plane, part], f"y{k}", y_peer).start()

    def grad_wide(plane, lhs, rhs):
        for j, target in ((1, gsend), (0, gown)):
            for at, size in cut(0, hidden, 256):
                left, right = lhs(j, slice(at, at + size)), rhs(j)
                target[plane, at : at + size, :] = dot(left, right, TN).astype(BF)
                if j == 1:
                    send_pieces(plane, at, at + size)

    def grad_down():
        grad_wide(0, lambda j, c: act[j, :, c], lambda j: gm[...])

    def grad_up():
        grad_wide(1, lambda j, c: n2[:, c], lambda j: gp[j])

    def grad_out():
        value = dot(att[...], ga[...], TN).astype(BF)
        gsend[2, 0:head_width, :] = value[head_width:, :]
        send_pieces(2, 0, head_width)
        gown[2, 0:head_width, :] = value[:head_width, :]

    ones = jnp.ones((16, length), BF)

    def grad_qkv():
        sums_up = [dot(ones, gp[j], NN)[0:1, :] for j in range(2)]
        sums_q = dot(ones, qb[...], NN)[0:1, :]
        sums_v = dot(ones, vb[...], NN)[0:1, :]
        lane = lax.broadcasted_iota(jnp.int32, (1, 2 * head_width), 1)
        for j, target in ((0, gown), (1, gsend)):
            mine = (lane < head_width) if j == 0 else (lane >= head_width)
            at = 4 * head_width
            row = lax.broadcasted_iota(jnp.int32, (16, 1), 0)
            pad = jnp.zeros((1, width - 2 * head_width), F32)
            q_row = jnp.concatenate([jnp.where(mine, sums_q, 0.0), pad], axis=1)
            v_row = jnp.concatenate([jnp.where(mine, sums_v, 0.0), pad], axis=1)
            block = jnp.where(
                row == 0, sums_up[j], jnp.where(row == 1, q_row, jnp.where(row == 2, v_row, 0.0))
            )
            target[2, at : at + 16, :] = block.astype(BF)
        for c, source in enumerate((qb, kb, vb)):
            value = dot(source[...], n1[...], TN).astype(BF)
            at = (c + 1) * head_width
            gsend[2, at : at + head_width, :] = value[head_width:, :]
            send_pieces(2, at, at + head_width)
            gown[2, at : at + head_width, :] = value[:head_width, :]

    @pl.when(early)
    def _():
        arrive(6, 7)
        finish_forward(True)
        for i, (at, size) in enumerate(own_rows):
            part = gm.at[pl.ds(at, size)]
            remote(part, part, f"g{i}", x_peer).wait_recv()
            share(gm, "gm", i).start()
        for i in range(2):
            share(gm, "gm", i).wait_recv()
        grad_down()
        for at, size, j, value in grad_active():
            r = slice(at, at + size)
            gp[j, r, :] = (value * gp[j, r, :].astype(F32)).astype(BF)
        for k in (6, 7):
            weight_relay(k, fresh).wait_send()
        offer(0)
        grad_up()

    for i in range(2):
        share(gm, "gm", i).wait_send()
    sums[5:6, :] = column_sum(gm[0:half, :].astype(F32))

    def grad_n2(r):
        return dot(gp[0, r, :], wub[0], NT) + dot(gp[1, r, :], wub[1], NT)

    for i, (at, size) in enumerate(own_rows):
        reduce_start(grad_n2(slice(half + at, half + at + size)), i, "o3", send_a, recv_a)
    added = [jnp.zeros((1, width), F32)] * 3
    for i, (at, size) in enumerate(own_rows):
        r = slice(at, at + size)
        grad = grad_n2(r) + reduce_end(i, "o3", send_a, recv_a)
        unit, scale = normalize(hid[r, :])
        grad_hidden = gm[r, :].astype(F32) + norm_back(grad, par[3:4, :], unit, scale)
        rounded = grad_hidden.astype(BF)
        gh[r, :] = grad_hidden
        ga[r, :] = rounded
        share(ga, "ga", i).start()
        added[0] = added[0] + column_sum(grad * unit)
        added[1] = added[1] + column_sum(grad)
        added[2] = added[2] + column_sum(rounded.astype(F32))
    for k in (4, 5):
        weight_relay(k, fresh).wait_send()
    offer(1)
    sums[3:4, :] = added[0]
    sums[4:5, :] = added[1]
    sums[2:3, :] = added[2]

    gatt[0:half, :] = dot(ga[0:half, :], wob[...], NT).astype(BF)
    for i in range(2):
        share(ga, "ga", i).wait_recv()
    gatt[half:, :] = dot(ga[half:, :], wob[...], NT).astype(BF)

    @pl.when(early)
    def _():
        grad_out()

    advance(early, (0,), ())
    for pair in range(pairs):
        cs = slice(pair * 2 * HD, (pair + 1) * 2 * HD)
        sum_k = jnp.zeros((length, 2 * HD), F32)
        sum_v = jnp.zeros((length, 2 * HD), F32)
        for at, size in both:
            r = slice(at, at + size)
            factors = [linv[r, 2 * pair + head : 2 * pair + head + 1] for head in range(2)]
            scaled = gatt[r, cs].astype(F32) * jnp.where(lane_mask(0), factors[0], factors[1])
            scaled = scaled.astype(BF)
            inner = scaled.astype(F32) * (att[r, cs].astype(F32) + att_rest[r, cs].astype(F32))
            queries = qb[r, cs]
            sum_q = jnp.zeros((size, 2 * HD), F32)
            for head in range(2):
                mask = lane_mask(head)
                level = jnp.sum(jnp.where(mask, inner, 0.0), axis=1, keepdims=True)
                grad = jnp.where(mask, scaled, zero)
                weights = prob[2 * pair + head, r, :]
                grad_scores = dot(grad, vb[:, cs], NT) - level
                grad_scores = (weights.astype(F32) * grad_scores).astype(BF)
                sum_v = sum_v + dot(weights, grad, TN)
                sum_k = sum_k + dot(grad_scores, jnp.where(mask, queries, zero), TN)
                sum_q = sum_q + dot(grad_scores, jnp.where(mask, kb[:, cs], zero), NN)
            qb[r, cs] = (sum_q * HD**-0.5).astype(BF)
        kb[:, cs] = sum_k.astype(BF)
        vb[:, cs] = sum_v.astype(BF)
        if pair == 0:
            advance(early, (1,), [("A", 0)])
        if pair == 1:
            advance(early, (2,), ())

    offer(2)
    advance(early, (), [("A", 1), ("M", 0)])

    def grad_n1(r):
        return (
            dot(qb[r, :], wqb[0], NN) + dot(kb[r, :], wqb[1], NN) + dot(vb[r, :], wqb[2], NN)
        )

    for i, (at, size) in enumerate(own_rows):
        reduce_start(grad_n1(slice(half + at, half + at + size)), i, "o4", send_a, recv_a)
    added = [jnp.zeros((1, width), F32)] * 4
    for i, (at, size) in enumerate(own_rows):
        r = slice(at, at + size)
        grad = grad_n1(r) + reduce_end(i, "o4", send_a, recv_a)
        unit, scale = normalize(xs[r, :])
        grad_input = gh[r, :] + norm_back(grad, par[0:1, :], unit, scale)
        gxb[r, :] = grad_input.astype(BF)

        @pl.when(late)
        def _():
            remote(gxb.at[r], gm.at[r], f"g{i}", x_peer).start()

        added[0] = added[0] + column_sum(grad * unit)
        added[1] = added[1] + column_sum(grad)
        added[2] = added[2] + column_sum(grad_input)
        added[3] = added[3] + column_sum(grad_input * xs[r, :])
    sums[0:1, :] = added[0]
    sums[1:2, :] = added[1]
    sums[6:7, :] = added[2]
    sums[7:8, :] = added[3]
    finish = share_out("b", sums, sumt, "t")
    local(gxb.at[pl.ds(0, rows)], sg.at[y], 7).start()

    advance(early, (3,), [("A", 2), ("M", 1)])

    @pl.when(early)
    def _():
        grad_qkv()

    @pl.when(late)
    def _():
        grad_down()
        grad_up()
        grad_out()
        grad_qkv()
        finish_forward(False)
        for k in (6, 7):
            weight_relay(k, fresh).wait_send()
        offer(0)

    remote(gxb.at[pl.ds(rows, rows)], sg.at[y], "sg", y_peer).start()
    wide = sum(plane < 2 for plane, _, _ in pieces)
    advance(early, range(4, wide), [("A", 3), ("M", 2), *steps(4, wide)])
    advance(late, range(wide), steps(0, wide))
    finish()
    sums[...] = jnp.sum(sumt[...], axis=0)
    finish = share_out("b", sums, sumz, "z")
    last = len(pieces)
    advance(early | late, range(wide, last), [*steps(wide, last), ("M", last - 1)])

    @pl.when(not_middle)
    def _():
        for k in range(last):
            receive(k)


    finish()
    small[0:8, :] = jnp.sum(sumz[...], axis=0)

    for k in range(len(pieces)):
        leave(k).wait()

        @pl.when(is_middle)
        def _():
            crossing(k).wait_send()

        @pl.when(not_middle)
        def _():
            inward(k).wait_send()

        @pl.when(not_end)
        def _():
            outward(k).wait_send()

    for i, (at, size) in enumerate(own_rows):
        for buffer, kind in ((n1, "n1"), (n2, "n2"), (ga, "ga")):
            share(buffer, kind, i).wait_send()
        part = pl.ds(at, size)

        @pl.when(early)
        def _():
            remote(obuf.at[part], obuf.at[part], f"x{i}", x_peer).wait_send()

        @pl.when(late)
        def _():
            remote(gxb.at[part], gm.at[part], f"g{i}", x_peer).wait_send()

    bias_copy.wait_send()
    for k in range(len(parts)):
        weight_copy(k).wait_send()
    for k in range(4):
        weight_relay(k, fresh).wait_send()
    remote(clips.at[0], in_dst, "in", y_peer).wait_send()
    local(obuf.at[pl.ds(0, rows)], states.at[y], 6).wait()
    local(gxb.at[pl.ds(0, rows)], sg.at[y], 7).wait()
    for source, target, name in ((obuf, states, "states"), (gxb, sg, "sg")):
        copy = remote(source.at[pl.ds(rows, rows)], target.at[1 - y], name, y_peer)
        copy.wait_send()
        copy.wait_recv()


def per_device(
    clips, group_clips, ln1_gain, ln1_bias, qkv_weight, q_bias, v_bias, out_weight, out_bias,
    ln2_gain, ln2_bias, up_weight, up_bias, down_weight, down_bias, cotangent,
    batches,
):
    _, rows, width = clips.shape
    head_width = q_bias.shape[1]
    hidden = up_bias.shape[1]
    half, length = 2 * rows, 4 * rows
    both_heads = 2 * head_width
    depth, pieces, index = plan(rows, width, head_width, hidden, batches)
    valid = (jnp.arange(2) < group_clips[0]).astype(F32)

    wq = jnp.transpose(qkv_weight[0], (1, 2, 0))
    nothing = jnp.zeros((1, width), F32)
    par = jnp.concatenate(
        [ln1_gain, ln1_bias, out_bias, ln2_gain, ln2_bias, down_bias, nothing, nothing]
    )

    def bias_rows(before, after):
        fill = jnp.zeros((1, before), F32), jnp.zeros((1, after), F32)
        rows_of = [jnp.concatenate([fill[0], v, fill[1]], axis=1) for v in (q_bias, v_bias)]
        return jnp.concatenate([up_bias, *rows_of, jnp.zeros((5, width), F32)])

    bias_own = bias_rows(0, width - head_width)
    bias_send = bias_rows(head_width, width - both_heads)
    valid_rows = jnp.zeros((8, 128), F32).at[:2].set(valid[:, None])

    vmem = pl.BlockSpec(memory_space=pltpu.VMEM)
    hbm = pl.BlockSpec(memory_space=pl.ANY)
    shape = jax.ShapeDtypeStruct

    def low(*dims):
        return pltpu.VMEM(dims, BF)

    def full(*dims):
        return pltpu.VMEM(dims, F32)

    scratch = [
        low(3, both_heads, width), low(both_heads, width),
        low(2, width, hidden), low(2, hidden, width), full(8, width),
        full(8, width), full(batches, 8, width), full(4, 8, width),
        full(8, width), full(batches, 8, width), full(4, 8, width),
        full(half, width), full(half, width), full(half, width), low(length, width),
        low(length, both_heads), low(length, both_heads), low(length, both_heads),
        low(both_heads // HD, length, length), full(length, 128), low(length, both_heads),
        low(length, both_heads),
        low(length, width), low(2, length, hidden), low(2, length, hidden),
        low(length, width), low(length, width), low(length, both_heads),
        low(half, width), low(half, width), low(half, width), low(half, width),
        low(half, width), low(half, width),
        low(3, depth, width), low(3, depth, width), low(3, depth, width),
        pltpu.SemaphoreType.DMA((len(index),)), pltpu.SemaphoreType.DMA((len(index),)),
        pltpu.SemaphoreType.DMA((8 + len(pieces),)), pltpu.SemaphoreType.REGULAR((3, 2)),
    ]
    dims = rows, width, head_width, hidden, batches, pieces, index
    grads, states, flow, small = pl.pallas_call(
        functools.partial(body, dims),
        out_shape=(
            shape((3, depth, width), BF),
            shape((2, rows, width), BF),
            shape((2, rows, width), BF),
            shape((16, width), F32),
        ),
        in_specs=[hbm] * 6 + [vmem] * 4,
        out_specs=(hbm, hbm, hbm, vmem),
        scratch_shapes=scratch,
        compiler_params=pltpu.CompilerParams(
            collective_id=0, has_side_effects=True, vmem_limit_bytes=64 * 2**20 - 2**17
        ),
        name="two_blocks",
    )(
        clips, cotangent, wq, out_weight[0], up_weight[0], down_weight[0],
        par, bias_own, bias_send, valid_rows,
    )

    mask = valid[:, None, None]
    center, inv_spread, total = small[8], small[9], small[10]
    flow = flow.astype(F32)
    standard = (clips.astype(F32) - center) * inv_spread
    raw = mask * inv_spread * (flow - small[6] / total - standard * (small[7] / total))
    flow = jnp.where(lax.axis_index("section") == 0, raw, flow)
    grads = grads.astype(F32)
    rest = grads[2]
    qkv = rest[head_width : 4 * head_width].reshape(3, head_width, width)
    ends = rest[4 * head_width :]
    q_grad = ends[1:2, :head_width] + ends[1:2, head_width:both_heads]
    v_grad = ends[2:3, :head_width] + ends[2:3, head_width:both_heads]
    return (
        (states * mask.astype(BF))[None],
        flow[None],
        small[0:1],
        small[1:2],
        jnp.transpose(qkv, (2, 0, 1))[None],
        q_grad,
        v_grad,
        rest[:head_width][None],
        small[2:3],
        small[3:4],
        small[4:5],
        grads[1, :width][None],
        ends[0:1, :hidden],
        grads[0, :hidden][None],
        small[5:6],
    )


def solution(mesh):
    section, tensor = P("section", None), P("section", "tensor")
    tokens, blocks = P("batch", "tensor", None), P("section", "batch", "tensor", None)
    columns, rows = P("section", None, "tensor"), P("section", "tensor", None)
    qkv = P("section", None, None, "tensor")
    return jax.shard_map(
        functools.partial(per_device, batches=mesh.shape["batch"]),
        mesh=mesh,
        in_specs=(
            tokens, P("batch"), section, section, qkv, tensor, tensor, rows, section,
            section, section, columns, tensor, rows, section, tokens,
        ),
        out_specs=(
            blocks, blocks, section, section, qkv, tensor, tensor, rows, section,
            section, section, columns, tensor, rows, section,
        ),
        check_vma=False,
    )
```

```python
import functools

import jax
import jax.numpy as jnp
from jax import lax
from jax.experimental import pallas as pl
from jax.experimental.pallas import tpu as pltpu
from jax.sharding import PartitionSpec as P

HD = 64
BF = jnp.bfloat16
F32 = jnp.float32
NN = (((1,), (0,)), ((), ()))
NT = (((1,), (1,)), ((), ()))
TN = (((0,), (0,)), ((), ()))
MESH = pl.DeviceIdType.MESH


def dot(a, b, dims):
    return lax.dot_general(a, b, dims, preferred_element_type=F32)


def cut(start, stop, step):
    return [(at, min(step, stop - at)) for at in range(start, stop, step)]


def lane_mask(head):
    lane = lax.broadcasted_iota(jnp.int32, (1, 2 * HD), 1)
    return lane < HD if head == 0 else lane >= HD


def normalize(v):
    shifted = v - jnp.mean(v, axis=-1, keepdims=True)
    scale = lax.rsqrt(jnp.mean(shifted * shifted, axis=-1, keepdims=True) + 1e-06)
    return shifted * scale, scale


def norm_back(g, gain, unit, scale):
    t = g * gain
    return scale * (
        t - jnp.mean(t, axis=-1, keepdims=True) - unit * jnp.mean(t * unit, axis=-1, keepdims=True)
    )


def column_sum(v):
    return jnp.sum(v, axis=0, keepdims=True)


def plan(width, head_width, hidden, batches):
    pieces = [(0, 0, hidden, at, size) for at, size in cut(0, width, 256)]
    pieces += [(1, at, size, 0, hidden) for at, size in cut(0, width, 256)]
    at = 0
    for size in (4, 4, 2, 2, 2, 1):
        pieces.append((2, at, size * head_width // 4, 0, width))
        at += size * head_width // 4
    pieces.append((2, at, 4 * head_width + 16 - at, 0, width))
    names = ["in", "bias", "states", "sg"]
    names += [f"{way}{k}" for way in ("wy", "wz") for k in range(10)]
    names += [f"{kind}{i}" for kind in ("n1", "x", "gm", "g") for i in range(4)]
    names += [f"{kind}{i}" for kind in ("n2", "ga", "o1", "o2", "o3", "o4") for i in range(2)]
    names += [f"{kind}{k}" for kind in ("y", "in", "out", "final") for k in range(len(pieces))]
    for stage in ("a", "b"):
        names += [f"{stage}z{j}" for j in range(1, batches)]
        names += [f"{stage}t{j}" for j in range(1, 4)]
    return pieces, {name: i for i, name in enumerate(names)}


def body(
    dims,
    clips, cot, wq, wo, wu, wd,
    gain1, offset1, shift_out, gain2, offset2, shift_down, q_bias, v_bias, up_bias, held,
    grad_d, grad_u, grad_r, states, sg, small,
    bias_send,
    wqb, wob, wub, wdb, bias_in, stat, statz, statt, sums, sumz, sumt,
    xs, hid, gh, n1, qb, kb, vb, prob, linv, att, att_rest, n2, act, gp, gm, ga, gatt,
    send_a, recv_a, recv_b, obuf, gown, gsend, grecv,
    ss, rs, ls, ready,
):
    rows, width, head_width, hidden, batches, pieces, index = dims
    half = 2 * rows
    length = 4 * rows
    heads = 2 * head_width // HD
    pairs = heads // 2
    section = lax.axis_index("section")
    b = lax.axis_index("batch")
    t = lax.axis_index("tensor")
    y, core = t // 2, t % 2
    core_peer = (section, b, 2 * y + 1 - core)
    y_peer = (section, b, 2 * (1 - y) + core)
    x_peer = (1 - section, b, t)
    early = section == 0
    late = section == 1

    def remote(src, dst, name, device, sent=None):
        i = index[name]
        return pltpu.make_async_remote_copy(
            src_ref=src, dst_ref=dst, send_sem=ss.at[index[sent or name]], recv_sem=rs.at[i],
            device_id=device, device_id_type=MESH,
        )

    def local(src, dst, i):
        return pltpu.make_async_copy(src, dst, ls.at[i])

    inb = recv_b
    gxb = prob.at[2, pl.ds(0, half), pl.ds(0, width)]
    own_loads = [
        local(clips.at[0], send_a.at[pl.ds(0, rows)], 0),
        local(wq, wqb.at[:, pl.ds(0, head_width)], 1),
        local(wo, wob.at[pl.ds(0, head_width)], 2),
        local(wu, wub.at[0], 3),
        local(wd, wdb.at[0], 4),
        local(clips.at[1], send_a.at[pl.ds(rows, rows)], 7),
    ]
    for k in (0, 5, 1, 2, 3, 4):
        own_loads[k].start()

    @pl.when(early)
    def _():
        local(clips.at[y], inb.at[pl.ds(0, rows)], 5).start()

    @pl.when(late)
    def _():
        local(cot.at[y], inb.at[pl.ds(0, rows)], 5).start()

    barrier = pltpu.get_barrier_semaphore()
    peers = [x_peer]
    peers += [(section, lax.rem(b + j, batches), t) for j in range(1, batches)]
    peers += [(section, b, lax.rem(t + j, 4)) for j in range(1, 4)]
    for peer in peers:
        pl.semaphore_signal(barrier, inc=1, device_id=peer, device_id_type=MESH)
    bias_send[...] = jnp.zeros((8, width), F32)
    bias_send[0:1, :hidden] = up_bias[...]
    bias_send[1:2, :head_width] = q_bias[...]
    bias_send[2:3, :head_width] = v_bias[...]
    in_dst = inb.at[pl.ds(rows, rows)]

    z_peer = (section, b + 1 - 2 * lax.rem(b, 2), t)
    fresh = lax.rem(b, 2)
    bias_copy = remote(bias_send, bias_in, "bias", y_peer)
    parts = []
    for source, target, at, size in (
        [(wq.at[c], lambda r, c=c: wqb.at[c, pl.ds(head_width + r[0], r[1])], 0, head_width) for c in range(3)]
        + [(wo, lambda r: wob.at[pl.ds(head_width + r[0], r[1])], 0, head_width)]
        + [(wu, lambda r: wub.at[1, pl.ds(*r)], at, width // 2) for at in (0, width // 2)]
        + [(wd, lambda r: wdb.at[1, pl.ds(*r)], at, size) for at, size in cut(0, hidden, hidden // 4)]
    ):
        parts.append((source, target, at, size // 2))

    def weight_rows(k, turn):
        _, _, at, size = parts[k]
        return pl.multiple_of(at + turn * size, 16), size

    def weight_copy(k):
        source, target, _, _ = parts[k]
        where = weight_rows(k, fresh)
        return remote(source.at[pl.ds(*where)], target(where), f"wy{k}", y_peer)

    def weight_relay(k, turn):
        place = parts[k][1](weight_rows(k, turn))
        return remote(place, place, f"wz{k}", z_peer)

    def relay(*which):
        for k in which:
            weight_copy(k).wait_recv()
            weight_relay(k, fresh).start()

    def arrive(*which):
        for k in which:
            weight_relay(k, 1 - fresh).wait_recv()

    def share_out(stage, block, slots, axis):
        size, me = (batches, b) if axis == "z" else (4, t)
        copies = []
        for j in range(1, size):
            to = lax.rem(me + j, size)
            device = (section, to, t) if axis == "z" else (section, b, to)
            copies.append(remote(block, slots.at[me], f"{stage}{axis}{j}", device))
        for copy in copies:
            copy.start()
        slots[pl.ds(me, 1)] = block[...][None]

        def finish():
            for j in range(1, size):
                origin = lax.rem(me + size - j, size)
                remote(block, slots.at[origin], f"{stage}{axis}{j}", core_peer).wait_recv()
            for copy in copies:
                copy.wait_send()

        return finish

    def store_stats(total, centered, count):
        stat[0:1, :] = total
        stat[1:2, :] = centered
        stat[2:3, :] = count
        stat[3:8, :] = jnp.zeros((5, width), F32)

    def merge_stats(slots):
        blocks = slots[...]
        total = jnp.sum(blocks[:, 0:1, :], axis=0)
        count = jnp.sum(blocks[:, 2:3, :], axis=0)
        away = blocks[:, 0, :] / blocks[:, 2, :] - total / count
        centered = jnp.sum(blocks[:, 1, :] + blocks[:, 2, :] * away * away, axis=0, keepdims=True)
        store_stats(total, centered, count)

    own_loads[0].wait()
    own_loads[5].wait()
    slots_of = [slice(m * rows, (m + 1) * rows) for m in range(2)]
    weight = [jnp.clip(held[0].astype(F32) - m, 0.0, 1.0) for m in range(2)]
    count = rows * (weight[0] + weight[1])
    total = jnp.zeros((1, width), F32)
    for m in range(2):
        total = total + weight[m] * column_sum(send_a[slots_of[m], :].astype(F32))
    centered = jnp.zeros((1, width), F32)
    for m in range(2):
        away = send_a[slots_of[m], :].astype(F32) - total / count
        centered = centered + weight[m] * column_sum(away * away)
    store_stats(total, centered, count + jnp.zeros((1, width), F32))
    pl.semaphore_wait(barrier, len(peers))
    finish = share_out("a", stat, statt, "t")
    bias_copy.start()

    @pl.when(early)
    def _():
        remote(clips.at[1 - y], in_dst, "in", y_peer).start()

    @pl.when(late)
    def _():
        remote(cot.at[1 - y], in_dst, "in", y_peer).start()

    for k in range(len(parts)):
        weight_copy(k).start()

    finish()
    merge_stats(statt)
    finish = share_out("a", stat, statz, "z")
    finish()
    merge_stats(statz)
    center = stat[0:1, :] / stat[2:3, :]
    inv_spread = lax.rsqrt(stat[1:2, :] / stat[2:3, :] + 1e-05)
    small[8:9, :] = center
    small[9:10, :] = inv_spread
    small[10:11, :] = stat[2:3, :]
    small[11:16, :] = jnp.zeros((5, width), F32)

    local(clips.at[y], inb.at[pl.ds(0, rows)], 5).wait()
    own_rows = cut(0, half, rows)
    quarters = cut(0, half, rows // 2)
    columns = cut(0, width, 256)

    def share(buffer, kind, i, chunks=own_rows):
        at, size = chunks[i]
        return remote(
            buffer.at[pl.ds(at, size)], buffer.at[pl.ds(half + at, size)], f"{kind}{i}", core_peer
        )

    def share_gm(i):
        c = pl.ds(*columns[i])
        return remote(gm.at[pl.ds(0, half), c], gm.at[pl.ds(half, half), c], f"gm{i}", core_peer)

    def grad_active():
        for at, size in ((0, half), (half, half)):
            for j in range(2):
                yield at, size, j, dot(gm[at : at + size, :], wdb[j], NT)

    own_loads[4].wait()

    @pl.when(early)
    def _():
        gp[...] = jnp.ones((2, length, hidden), BF)

    @pl.when(late)
    def _():
        remote(clips.at[0], in_dst, "in", y_peer).wait_recv()
        mine = jnp.clip(held[0].astype(F32) - y.astype(F32), 0.0, 1.0)
        for at, size in own_rows:
            gm[at : at + size, :] = (inb[at : at + size, :].astype(F32) * mine).astype(BF)
        for i in range(len(columns)):
            share_gm(i).start()
        relay(*range(10))
        arrive(6, 7, 8, 9)
        for i in range(len(columns)):
            share_gm(i).wait_recv()
        for at, size, j, value in grad_active():
            gp[j, at : at + size, :] = value.astype(BF)

    def norm_one(i, first):
        at, size = quarters[i]
        r = slice(at, at + size)
        if first:
            if at == rows:
                remote(clips.at[0], in_dst, "in", y_peer).wait_recv()
            xs[r, :] = (inb[r, :].astype(F32) - center) * inv_spread
        else:
            remote(obuf.at[r], obuf.at[r], f"x{i}", x_peer).wait_recv()
            xs[r, :] = obuf[r, :].astype(F32)
        unit, _ = normalize(xs[r, :])
        n1[r, :] = (unit * gain1[...] + offset1[...]).astype(BF)
        share(n1, "n1", i, quarters).start()

    def project(r, shift_q, shift_v):
        normed = n1[r, :]
        queries = (dot(normed, wqb[0], NT) + shift_q).astype(BF)
        qb[r, :] = queries * jnp.array(HD**-0.5, BF)
        kb[r, :] = dot(normed, wqb[1], NT).astype(BF)
        vb[r, :] = (dot(normed, wqb[2], NT) + shift_v).astype(BF)

    @pl.when(early)
    def _():
        for i in range(4):
            norm_one(i, True)
        relay(0, 1, 2, 3)

    @pl.when(late)
    def _():
        norm_one(0, False)
        norm_one(1, False)

    own_loads[1].wait()
    bias_copy.wait_recv()
    shifts = [
        jnp.concatenate([bias_send[i : i + 1, :head_width], bias_in[i : i + 1, :head_width]], axis=1)
        for i in (1, 2)
    ]
    arrive(0, 1, 2)
    project(slice(0, rows), *shifts)
    for i in range(2):
        share(n1, "n1", i, quarters).wait_recv()
    project(slice(half, half + rows), *shifts)

    @pl.when(late)
    def _():
        norm_one(2, False)
        norm_one(3, False)

    project(slice(rows, half), *shifts)
    for i in range(2, 4):
        share(n1, "n1", i, quarters).wait_recv()
    project(slice(half + rows, length), *shifts)

    zero = jnp.zeros((), BF)

    def attend(at, size, pair):
        r = slice(at, at + size)
        cs = slice(pair * 2 * HD, (pair + 1) * 2 * HD)
        outs = []
        for head in range(2):
            mask = lane_mask(head)
            scores = dot(jnp.where(mask, qb[r, cs], zero), kb[:, cs], NT)
            exponent = jnp.exp(scores - jnp.max(scores, axis=1, keepdims=True)).astype(BF)
            prob[2 * pair + head, r, :] = exponent
            first = HD * (1 - head)
            lane = lax.broadcasted_iota(jnp.int32, (1, 2 * HD), 1)
            ones = jnp.where(lane == first, jnp.ones((), BF), zero)
            result = dot(exponent, jnp.where(mask, vb[:, cs], ones), NN)
            factor = 1.0 / result[:, first : first + 1]
            linv[r, 2 * pair + head : 2 * pair + head + 1] = factor
            outs.append(result * factor)
        exact = jnp.where(lane_mask(0), outs[0], outs[1])
        near = exact.astype(BF)
        att[r, cs] = near
        att_rest[r, cs] = (exact - near.astype(F32)).astype(BF)

    def reduce_start(value, i, name, send, recv):
        at, size = own_rows[i]
        send[at : at + size, :] = value.astype(BF)
        remote(send.at[pl.ds(at, size)], recv.at[pl.ds(at, size)], f"{name}{i}", core_peer).start()

    def reduce_end(i, name, send, recv):
        at, size = own_rows[i]
        remote(send.at[pl.ds(at, size)], recv.at[pl.ds(at, size)], f"{name}{i}", core_peer).wait()
        return recv[at : at + size, :].astype(F32)

    for pair in range(pairs):
        attend(half, half, pair)
        if pair == 1:

            @pl.when(early)
            def _():
                relay(4)

    own_loads[2].wait()
    arrive(3)
    for i, (at, size) in enumerate(own_rows):
        reduce_start(dot(att[half + at : half + at + size, :], wob[...], NN), i, "o1", send_a, recv_a)

    for pair in range(pairs):
        attend(0, half, pair)

    @pl.when(early)
    def _():
        relay(5)

    for i, (at, size) in enumerate(own_rows):
        r = slice(at, at + size)
        partial = dot(att[r, :], wob[...], NN)
        hidden_rows = xs[r, :] + (partial + reduce_end(i, "o1", send_a, recv_a) + shift_out[...])
        hid[r, :] = hidden_rows
        unit, _ = normalize(hidden_rows)
        n2[r, :] = (unit * gain2[...] + offset2[...]).astype(BF)
        share(n2, "n2", i).start()

    def up(j, r):
        before = dot(n2[r, :], wub[j], NN) + (bias_send if j == 0 else bias_in)[0:1, :hidden]
        share_of = 0.5 + 0.5 * lax.erf(before * (2.0**-0.5))
        act[j, r, :] = (before * share_of).astype(BF)
        slope = share_of + before * jnp.exp(-0.5 * before * before) * 0.3989422804014327
        gp[j, r, :] = (gp[j, r, :].astype(F32) * slope).astype(BF)

    @pl.when(early)
    def _():
        relay(6)

    own_loads[3].wait()
    up(0, slice(0, half))
    for i in range(2):
        share(n2, "n2", i).wait_recv()
    up(0, slice(half, length))

    @pl.when(early)
    def _():
        relay(7)

    arrive(4, 5)
    up(1, slice(0, half))
    up(1, slice(half, length))

    @pl.when(early)
    def _():
        relay(8, 9)

    def down(r):
        return dot(act[0, r, :], wdb[0], NN) + dot(act[1, r, :], wdb[1], NN)

    def finish_forward(send_on):
        for i, (at, size) in enumerate(own_rows):
            reduce_start(down(slice(half + at, half + at + size)), i, "o2", send_a, recv_b)
        for i, (at, size) in enumerate(own_rows):
            r = slice(at, at + size)
            value = down(r) + reduce_end(i, "o2", send_a, recv_b) + shift_down[...]
            obuf[r, :] = (hid[r, :] + value).astype(BF)
            if send_on:
                for q in (2 * i, 2 * i + 1):
                    part = obuf.at[pl.ds(*quarters[q])]
                    remote(part, part, f"x{q}", x_peer).start()

        local(obuf.at[pl.ds(0, rows)], states.at[y], 6).start()
        remote(obuf.at[pl.ds(rows, rows)], states.at[y], "states", y_peer).start()

    inner = jnp.where(b < batches // 2, b + 1, b - 1)
    outer = jnp.where(b < batches // 2, b - 1, b + 1)
    inner_peer, outer_peer = (section, inner, t), (section, outer, t)
    is_end = jnp.logical_or(b == 0, b == batches - 1)
    is_middle = jnp.logical_or(b == batches // 2 - 1, b == batches // 2)
    not_end, not_middle = jnp.logical_not(is_end), jnp.logical_not(is_middle)

    firsts = [min(k for k, piece in enumerate(pieces) if piece[0] == plane) for plane in range(3)]
    wide = firsts[2]
    last = len(pieces)

    def offer(plane):
        @pl.when(is_middle)
        def _():
            pl.semaphore_signal(ready.at[plane, 0], inc=1, device_id=inner_peer, device_id_type=MESH)

        @pl.when(not_middle)
        def _():
            pl.semaphore_signal(ready.at[plane, 1], inc=1, device_id=inner_peer, device_id_type=MESH)

        @pl.when(not_end)
        def _():
            pl.semaphore_signal(ready.at[plane, 0], inc=1, device_id=outer_peer, device_id_type=MESH)

    def place(k):
        plane, at, size, left, wide = pieces[k]
        return plane, pl.ds(at, size), pl.ds(left, wide)

    def slot(k, outside):
        plane, r, c = place(k)
        return (act, wub, prob)[plane].at[outside, r, c]

    def block(ref, k):
        return ref.at[place(k)]

    def crossing(k):
        return remote(block(gown, k), slot(k, 0), f"in{k}", inner_peer)

    def inward(k):
        return remote(block(gown, k), slot(k, 1), f"out{k}", inner_peer)

    def outward(k):
        return remote(slot(k, 0), slot(k, 0), f"in{k}", outer_peer, f"final{k}")

    def leave(k):
        plane, r, c = place(k)
        return local(slot(k, 0), (grad_d, grad_u, grad_r)[plane].at[r, c], 8 + k)

    def send_chip(k):
        return remote(block(gsend, k), block(grecv, k), f"y{k}", y_peer)

    def add_chips(k):
        plane = pieces[k][0]
        send_chip(k).wait()
        chip = block(gown, k)[...].astype(F32) + block(grecv, k)[...].astype(F32)

        @pl.when(is_end)
        def _():
            block(gown, k)[...] = chip.astype(BF)

        @pl.when(not_end)
        def _():
            inward(k).wait_recv()
            block(gown, k)[...] = (chip + slot(k, 1)[...].astype(F32)).astype(BF)

        if k == firsts[plane]:
            pl.semaphore_wait(ready.at[plane, 0], 1)

            @pl.when(not_end)
            def _():
                pl.semaphore_wait(ready.at[plane, 1], 1)

        @pl.when(is_middle)
        def _():
            crossing(k).start()

        @pl.when(not_middle)
        def _():
            inward(k).start()

    def pass_on(k):
        @pl.when(not_end)
        def _():
            outward(k).start()

        leave(k).start()

    def add_middle(k):
        crossing(k).wait_recv()
        value = block(gown, k)[...].astype(F32) + slot(k, 0)[...].astype(F32)
        slot(k, 0)[...] = value.astype(BF)
        pass_on(k)

    def receive(k):
        crossing(k).wait_recv()
        pass_on(k)

    def advance(where, at_ends, inside):
        if len(at_ends):

            @pl.when(is_end if where is True else jnp.logical_and(where, is_end))
            def _():
                for k in at_ends:
                    add_chips(k)

        if len(inside):

            @pl.when(not_end if where is True else jnp.logical_and(where, not_end))
            def _():
                for kind, k in inside:
                    if kind == "A":
                        add_chips(k)
                    else:

                        @pl.when(is_middle)
                        def _():
                            add_middle(k)

    def steps(start, stop, lag=1):
        found = []
        for k in range(start, stop):
            found.append(("A", k))
            if k >= lag:
                found.append(("M", k - lag))
        return found

    def grad_down(j, i):
        left, wide = columns[i]
        c = slice(left, left + wide)
        for at, size in cut(0, hidden, 256):
            value = dot(act[j, :, at : at + size], gm[:, c], TN).astype(BF)
            (gown, gsend)[j][0, at : at + size, c] = value
        if j == 1:
            send_chip(firsts[0] + i).start()

    def grad_up(j):
        for i, (at, size) in enumerate(cut(0, width, 256)):
            value = dot(n2[:, at : at + size], gp[j], TN).astype(BF)
            (gown, gsend)[j][1, at : at + size, :] = value
            if j == 1:
                send_chip(firsts[1] + i).start()

    def send_rest(start, stop):
        for k in range(firsts[2], last):
            if start <= pieces[k][1] < stop:
                send_chip(k).start()

    def grad_out():
        value = dot(att[...], ga[...], TN).astype(BF)
        gsend[2, 0:head_width, :] = value[head_width:, :]
        send_rest(0, head_width)
        gown[2, 0:head_width, :] = value[:head_width, :]

    ones = jnp.ones((16, length), BF)

    def grad_qkv():
        sums_up = [dot(ones, gp[j], NN)[0:1, :] for j in range(2)]
        sums_q = dot(ones, qb[...], NN)[0:1, :]
        sums_v = dot(ones, vb[...], NN)[0:1, :]
        lane = lax.broadcasted_iota(jnp.int32, (1, 2 * head_width), 1)
        for j, target in ((0, gown), (1, gsend)):
            mine = (lane < head_width) if j == 0 else (lane >= head_width)
            at = 4 * head_width
            row = lax.broadcasted_iota(jnp.int32, (16, 1), 0)
            pad = jnp.zeros((1, width - 2 * head_width), F32)
            q_row = jnp.concatenate([jnp.where(mine, sums_q, 0.0), pad], axis=1)
            v_row = jnp.concatenate([jnp.where(mine, sums_v, 0.0), pad], axis=1)
            block = jnp.where(
                row == 0, sums_up[j], jnp.where(row == 1, q_row, jnp.where(row == 2, v_row, 0.0))
            )
            target[2, at : at + 16, :] = block.astype(BF)
        for c, source in enumerate((qb, kb, vb)):
            value = dot(source[...], n1[...], TN).astype(BF)
            at = (c + 1) * head_width
            gsend[2, at : at + head_width, :] = value[head_width:, :]
            send_rest(at, at + head_width)
            gown[2, at : at + head_width, :] = value[:head_width, :]

    @pl.when(early)
    def _():
        arrive(6, 7, 8, 9)
        finish_forward(True)
        for i in range(len(columns)):
            part = gm.at[pl.ds(0, half), pl.ds(*columns[i])]
            remote(part, part, f"g{i}", x_peer).wait_recv()
            share_gm(i).start()
            if i:
                share_gm(i - 1).wait_recv()
                grad_down(1, i - 1)
        share_gm(len(columns) - 1).wait_recv()
        grad_down(1, len(columns) - 1)
        for i in range(len(columns)):
            grad_down(0, i)
        offer(0)
        advance(True, (0,), ())
        for at, size, j, value in grad_active():
            r = slice(at, at + size)
            gp[j, r, :] = (value * gp[j, r, :].astype(F32)).astype(BF)

    for i in range(len(columns)):
        share_gm(i).wait_send()
    sums[5:6, :] = column_sum(gm[0:half, :].astype(F32))

    def grad_n2(r):
        return dot(gp[0, r, :], wub[0], NT) + dot(gp[1, r, :], wub[1], NT)

    for i, (at, size) in enumerate(own_rows):
        reduce_start(grad_n2(slice(half + at, half + at + size)), i, "o3", send_a, recv_a)

    @pl.when(early)
    def _():
        grad_up(1)
        advance(True, (1,), ())

    added = [jnp.zeros((1, width), F32)] * 3
    for i, (at, size) in enumerate(own_rows):
        r = slice(at, at + size)
        grad = grad_n2(r) + reduce_end(i, "o3", send_a, recv_a)
        unit, scale = normalize(hid[r, :])
        grad_hidden = gm[r, :].astype(F32) + norm_back(grad, gain2[...], unit, scale)
        rounded = grad_hidden.astype(BF)
        gh[r, :] = grad_hidden
        ga[r, :] = rounded
        share(ga, "ga", i).start()
        added[0] = added[0] + column_sum(grad * unit)
        added[1] = added[1] + column_sum(grad)
        added[2] = added[2] + column_sum(rounded.astype(F32))
    for k in (4, 5):
        weight_relay(k, fresh).wait_send()
    offer(1)
    sums[3:4, :] = added[0]
    sums[4:5, :] = added[1]
    sums[2:3, :] = added[2]

    @pl.when(early)
    def _():
        grad_up(0)
        advance(True, (), [("A", 0)])

    gatt[0:half, :] = dot(ga[0:half, :], wob[...], NT).astype(BF)
    for i in range(2):
        share(ga, "ga", i).wait_recv()
    gatt[half:, :] = dot(ga[half:, :], wob[...], NT).astype(BF)

    @pl.when(early)
    def _():
        grad_out()

    advance(early, (2,), ())
    for pair in range(pairs):
        cs = slice(pair * 2 * HD, (pair + 1) * 2 * HD)
        sum_k = jnp.zeros((length, 2 * HD), F32)
        sum_v = jnp.zeros((length, 2 * HD), F32)
        for at, size in ((0, half), (half, half)):
            r = slice(at, at + size)
            factors = [linv[r, 2 * pair + head : 2 * pair + head + 1] for head in range(2)]
            scaled = gatt[r, cs].astype(F32) * jnp.where(lane_mask(0), factors[0], factors[1])
            scaled = scaled.astype(BF)
            inner = scaled.astype(F32) * (att[r, cs].astype(F32) + att_rest[r, cs].astype(F32))
            queries = qb[r, cs]
            sum_q = jnp.zeros((size, 2 * HD), F32)
            for head in range(2):
                mask = lane_mask(head)
                level = jnp.sum(jnp.where(mask, inner, 0.0), axis=1, keepdims=True)
                grad = jnp.where(mask, scaled, zero)
                weights = prob[2 * pair + head, r, :]
                grad_scores = dot(grad, vb[:, cs], NT) - level
                grad_scores = (weights.astype(F32) * grad_scores).astype(BF)
                sum_v = sum_v + dot(weights, grad, TN)
                sum_k = sum_k + dot(grad_scores, jnp.where(mask, queries, zero), TN)
                sum_q = sum_q + dot(grad_scores, jnp.where(mask, kb[:, cs], zero), NN)
            qb[r, cs] = (sum_q * HD**-0.5).astype(BF)
        kb[:, cs] = sum_k.astype(BF)
        vb[:, cs] = sum_v.astype(BF)
        if pair == 0:
            advance(early, (), [("A", 1)])
        if pair == 1:
            advance(early, (3,), [("M", 0)])

    offer(2)
    advance(early, (), [("A", 2)])

    def grad_n1(r):
        return (
            dot(qb[r, :], wqb[0], NN) + dot(kb[r, :], wqb[1], NN) + dot(vb[r, :], wqb[2], NN)
        )

    for i, (at, size) in enumerate(own_rows):
        reduce_start(grad_n1(slice(half + at, half + at + size)), i, "o4", send_a, recv_a)

    @pl.when(early)
    def _():
        grad_qkv()
        advance(True, (4,), [("M", 1)])

    added = [jnp.zeros((1, width), F32)] * 4
    for i, (at, size) in enumerate(own_rows):
        r = slice(at, at + size)
        grad = grad_n1(r) + reduce_end(i, "o4", send_a, recv_a)
        unit, scale = normalize(xs[r, :])
        grad_input = gh[r, :] + norm_back(grad, gain1[...], unit, scale)
        gxb[r, :] = grad_input.astype(BF)
        added[0] = added[0] + column_sum(grad * unit)
        added[1] = added[1] + column_sum(grad)
        added[2] = added[2] + column_sum(grad_input)
        added[3] = added[3] + column_sum(grad_input * xs[r, :])

    def flow_back(i):
        c = pl.ds(*columns[i])
        return remote(gxb.at[pl.ds(0, half), c], gm.at[pl.ds(0, half), c], f"g{i}", x_peer)

    @pl.when(late)
    def _():
        for i in range(len(columns)):
            flow_back(i).start()

    sums[0:1, :] = added[0]
    sums[1:2, :] = added[1]
    sums[6:7, :] = added[2]
    sums[7:8, :] = added[3]
    finish = share_out("b", sums, sumt, "t")
    local(gxb.at[pl.ds(0, rows)], sg.at[y], 7).start()
    @pl.when(late)
    def _():
        for i in range(len(columns)):
            grad_down(1, i)
        grad_up(1)
        for i in range(len(columns)):
            grad_down(0, i)
        finish_forward(False)
        offer(0)
        grad_up(0)
        advance(True, (0,), ())
        grad_out()
        grad_qkv()
        advance(True, (1,), [("A", 0)])

    remote(gxb.at[pl.ds(rows, rows)], sg.at[y], "sg", y_peer).start()
    advance(early, range(5, wide), steps(3, wide))
    advance(late, range(2, wide), steps(1, wide))
    finish()
    sums[...] = jnp.sum(sumt[...], axis=0)
    finish = share_out("b", sums, sumz, "z")
    advance(True, range(wide, last), [*steps(wide, last), ("M", last - 1)])

    @pl.when(not_middle)
    def _():
        for k in range(last):
            receive(k)

    finish()
    small[0:8, :] = jnp.sum(sumz[...], axis=0)

    for k in range(len(pieces)):
        leave(k).wait()

        @pl.when(is_middle)
        def _():
            crossing(k).wait_send()

        @pl.when(not_middle)
        def _():
            inward(k).wait_send()

        @pl.when(not_end)
        def _():
            outward(k).wait_send()

    for i in range(2):
        share(n2, "n2", i).wait_send()
        share(ga, "ga", i).wait_send()
    for i in range(4):
        share(n1, "n1", i, quarters).wait_send()

    @pl.when(early)
    def _():
        for i in range(4):
            part = obuf.at[pl.ds(*quarters[i])]
            remote(part, part, f"x{i}", x_peer).wait_send()

    @pl.when(late)
    def _():
        for i in range(len(columns)):
            flow_back(i).wait_send()

    bias_copy.wait_send()
    for k in range(len(parts)):
        weight_copy(k).wait_send()
    for k in (0, 1, 2, 3, 6, 7, 8, 9):
        weight_relay(k, fresh).wait_send()
    remote(clips.at[0], in_dst, "in", y_peer).wait_send()
    local(obuf.at[pl.ds(0, rows)], states.at[y], 6).wait()
    local(gxb.at[pl.ds(0, rows)], sg.at[y], 7).wait()
    for source, target, name in ((obuf, states, "states"), (gxb, sg, "sg")):
        copy = remote(source.at[pl.ds(rows, rows)], target.at[1 - y], name, y_peer)
        copy.wait_send()
        copy.wait_recv()


def finish_outputs(
    head_width,
    states, flow, clips, grad_d, grad_u, grad_r, small, held,
    states_out, flow_out, d_out, u_out, qkv_out, out_out, *lines,
):
    some = head_width // 4
    at = pl.program_id(0) * some
    first = lax.axis_index("section") == 0
    center, scale, count = small[8:9, :], small[9:10, :], small[10:11, :]
    mean, cross = small[6:7, :] / count, small[7:8, :] / count
    for m in range(2):
        mask = jnp.clip(held[0].astype(F32) - m, 0.0, 1.0)
        states_out[m] = (states[m].astype(F32) * mask).astype(BF)
        grad = flow[m].astype(F32)
        standard = (clips[m].astype(F32) - center) * scale
        flow_out[m] = jnp.where(first, mask * scale * (grad - mean - standard * cross), grad)
    d_out[...] = grad_d[...].astype(F32)
    u_out[...] = grad_u[...].astype(F32)
    out_out[...] = grad_r[pl.ds(pl.multiple_of(at, 16), some), :].astype(F32)
    for c in range(3):
        start = pl.multiple_of((c + 1) * head_width + at, 16)
        qkv_out[c] = grad_r[pl.ds(start, some), :].astype(F32)
    for i in range(6):
        lines[i][...] = small[i : i + 1, :]
    ends = grad_r[4 * head_width :, :].astype(F32)
    lines[6][...] = ends[0:1, : lines[6].shape[1]]
    for i in (1, 2):
        lines[6 + i][...] = ends[i : i + 1, :head_width] + ends[i : i + 1, head_width : 2 * head_width]


def per_device(
    clips, group_clips, ln1_gain, ln1_bias, qkv_weight, q_bias, v_bias, out_weight, out_bias,
    ln2_gain, ln2_bias, up_weight, up_bias, down_weight, down_bias, cotangent,
    batches,
):
    _, rows, width = clips.shape
    head_width = q_bias.shape[1]
    hidden = up_bias.shape[1]
    half, length = 2 * rows, 4 * rows
    both_heads = 2 * head_width
    depth = max(hidden, 4 * head_width + 16)
    pieces, index = plan(width, head_width, hidden, batches)
    wq = jnp.transpose(qkv_weight[0], (1, 2, 0))

    vmem = pl.BlockSpec(memory_space=pltpu.VMEM)
    hbm = pl.BlockSpec(memory_space=pl.ANY)
    shape = jax.ShapeDtypeStruct

    def low(*dims):
        return pltpu.VMEM(dims, BF)

    def full(*dims):
        return pltpu.VMEM(dims, F32)

    scratch = [
        full(8, width),
        low(3, both_heads, width), low(both_heads, width),
        low(2, width, hidden), low(2, hidden, width), full(8, width),
        full(8, width), full(batches, 8, width), full(4, 8, width),
        full(8, width), full(batches, 8, width), full(4, 8, width),
        full(half, width), full(half, width), full(half, width), low(length, width),
        low(length, both_heads), low(length, both_heads), low(length, both_heads),
        low(both_heads // HD, length, length), full(length, 128), low(length, both_heads),
        low(length, both_heads),
        low(length, width), low(2, length, hidden), low(2, length, hidden),
        low(length, width), low(length, width), low(length, both_heads),
        low(half, width), low(half, width), low(half, width), low(half, width),
        low(3, depth, width), low(3, depth, width), low(3, depth, width),
        pltpu.SemaphoreType.DMA((len(index),)), pltpu.SemaphoreType.DMA((len(index),)),
        pltpu.SemaphoreType.DMA((8 + len(pieces),)), pltpu.SemaphoreType.REGULAR((3, 2)),
    ]
    dims = rows, width, head_width, hidden, batches, pieces, index
    grad_d, grad_u, grad_r, states, flow, small = pl.pallas_call(
        functools.partial(body, dims),
        out_shape=(
            shape((hidden, width), BF),
            shape((width, hidden), BF),
            shape((4 * head_width + 16, width), BF),
            shape((2, rows, width), BF),
            shape((2, rows, width), BF),
            shape((16, width), F32),
        ),
        in_specs=[hbm] * 6 + [vmem] * 9 + [pl.BlockSpec(memory_space=pltpu.SMEM)],
        out_specs=(hbm, hbm, hbm, hbm, hbm, vmem),
        scratch_shapes=scratch,
        compiler_params=pltpu.CompilerParams(
            collective_id=0, has_side_effects=True, vmem_limit_bytes=64 * 2**20 - 2**17
        ),
        name="two_blocks",
    )(
        clips, cotangent, wq, out_weight[0], up_weight[0], down_weight[0],
        ln1_gain, ln1_bias, out_bias, ln2_gain, ln2_bias, down_bias, q_bias, v_bias, up_bias, group_clips,
    )

    turns = 4
    some = rows // turns
    constant = (lambda i: (0, 0)), (lambda i: (i, 0)), (lambda i: (0, i, 0))
    tokens = pl.BlockSpec((2, some, width), constant[2])
    matrix_d = pl.BlockSpec((hidden // turns, width), constant[1])
    matrix_u = pl.BlockSpec((width // turns, hidden), constant[1])
    line = pl.BlockSpec((1, width), constant[0])
    heads_line = pl.BlockSpec((1, head_width), constant[0])
    ended = pl.pallas_call(
        functools.partial(finish_outputs, head_width),
        grid=(turns,),
        out_shape=(
            shape((2, rows, width), BF), shape((2, rows, width), F32),
            shape((hidden, width), F32), shape((width, hidden), F32),
            shape((3, head_width, width), F32), shape((head_width, width), F32),
            *[shape((1, width), F32)] * 6, shape((1, hidden), F32), *[shape((1, head_width), F32)] * 2,
        ),
        in_specs=[
            tokens, tokens, tokens, matrix_d, matrix_u,
            pl.BlockSpec(grad_r.shape, constant[0]), pl.BlockSpec((16, width), constant[0]),
            pl.BlockSpec(memory_space=pltpu.SMEM),
        ],
        out_specs=(
            tokens, tokens, matrix_d, matrix_u,
            pl.BlockSpec((3, head_width // turns, width), constant[2]),
            pl.BlockSpec((head_width // turns, width), constant[1]),
            *[line] * 6, pl.BlockSpec((1, hidden), constant[0]), heads_line, heads_line,
        ),
        compiler_params=pltpu.CompilerParams(vmem_limit_bytes=64 * 2**20 - 2**17),
        name="outputs",
    )(states, flow, clips, grad_d, grad_u, grad_r, small, group_clips)
    states, flow, grad_d, grad_u, qkv, grad_out, *lines, up_grad, q_grad, v_grad = ended
    return (
        states[None],
        flow[None],
        lines[0],
        lines[1],
        jnp.transpose(qkv, (2, 0, 1))[None],
        q_grad,
        v_grad,
        grad_out[None],
        lines[2],
        lines[3],
        lines[4],
        grad_u[None],
        up_grad,
        grad_d[None],
        lines[5],
    )


def solution(mesh):
    section, tensor = P("section", None), P("section", "tensor")
    tokens, blocks = P("batch", "tensor", None), P("section", "batch", "tensor", None)
    columns, rows = P("section", None, "tensor"), P("section", "tensor", None)
    qkv = P("section", None, None, "tensor")
    return jax.shard_map(
        functools.partial(per_device, batches=mesh.shape["batch"]),
        mesh=mesh,
        in_specs=(
            tokens, P("batch"), section, section, qkv, tensor, tensor, rows, section,
            section, section, columns, tensor, rows, section, tokens,
        ),
        out_specs=(
            blocks, blocks, section, section, qkv, tensor, tensor, rows, section,
            section, section, columns, tensor, rows, section,
        ),
        check_vma=False,
    )
```
